32 devices in a mesh: gx: 8 (over z, y), gy: 4 (over x, core).
Axes of the slice: x: 2, y: 2, z: 4, core: 2. Of those that a mesh axis runs over, the one named last changes fastest.
Arguments:
- cotangent: float32 [9, 64, 256, 256], P(None, 'gx', 'gy'), may hold values from -6 to 6
- fields_one: float32 [9, 64, 256, 256], P(None, 'gx', 'gy'), may hold values from 0 to 1
- fields_zero: float32 [9, 64, 256, 256], P(None, 'gx', 'gy'), may hold values from 0 to 1
- slot_grain: int32 [8, 32, 8], P('gx', 'gy'), may hold values from 0 to 255, as said below
Outputs:
- adjoint_fields: float32 [9, 64, 256, 256], P(None, 'gx', 'gy')
- grain_grad: float32 [256, 256], P(('gx', 'gy'))
The draws below stay inside these ranges and needn't reach their ends.
Inputs may be any that keep to these rules, and one draw needn't show every extreme that they name: `slot_grain`: grain g is owned by device g // 8, devices counted with gx slowest. Every slot of a tile names a grain whose owner has the tile's index along gy. At most 16 of the slots of one device name grains of one owner, and in every draw some owner receives exactly 16 from every device of its gy group.
All inputs are finite; a program needn't handle non-finite values.
Results may differ from the reference program's by a relative error of at most 0.000096.
Values sent between devices are 32-bit elements; how exact they have to be, the bound alone decides.
A program may use at most 128 MiB of HBM per device.

```python
import jax
import jax.numpy as jnp
from jax import lax

SLOTS = 8
TILE = 8
CX = 8
CY = 64
NZ = 256
GRAIN_DEV = 8
NX = 64
NY = 256
GRAINS = 256
ROWS_DEV = 64
CAP = 16
N_GX = 8
N_GY = 4


def draw_slot_grain(key, part):
    peer_count = N_GX
    groups = N_GY
    key_full, key_rows, key_local = jax.random.split(key, 3)
    full_peer = jax.random.randint(key_full, (groups,), 0, peer_count)
    full_each = jnp.tile(full_peer, peer_count)

    def one_device(device_key, chosen_peer):
        key_rank, key_shuffle = jax.random.split(device_key)
        ranks = jax.random.permutation(key_rank, peer_count * CAP)
        candidate = jnp.arange(peer_count * CAP)
        scores = ranks + jnp.where(candidate // CAP == chosen_peer, peer_count * CAP, 0)
        scores_top, picked = lax.top_k(scores, ROWS_DEV)
        picked = jax.random.permutation(key_shuffle, picked)
        return picked // CAP
    device_keys = jax.random.split(key_rows, peer_count * groups)
    peers = jax.vmap(one_device)(device_keys, full_each)
    local_id = jax.random.randint(key_local, (peer_count * groups, ROWS_DEV), 0, GRAIN_DEV)
    group_index = jnp.arange(peer_count * groups) % groups
    grains = (peers * groups + group_index[:, None]) * GRAIN_DEV + local_id
    grains = grains.reshape(peer_count, groups, CX // TILE, CY // TILE, SLOTS)
    grains = jnp.transpose(grains, (0, 2, 1, 3, 4))
    return grains.reshape(NX // TILE, NY // TILE, SLOTS).astype(jnp.int32)


def levels(own_key, dims, shards, low, largest):
    factor_of, own = 1.0, jax.random.fold_in(own_key, 6)
    for position, parts in shards:
        draws = jnp.exp(jax.random.uniform(jax.random.fold_in(own, position), (parts,), jnp.float32, low / len(shards), largest / len(shards)))
        factor_of = factor_of * jnp.repeat(draws, dims[position] // parts).reshape([-1 if axis == position else 1 for axis in range(len(dims))])
    return factor_of


def gaussian(stream_key, extent, spread, limit, shards=(), kind=jnp.bfloat16):
    drawn = spread * jax.random.normal(stream_key, extent, jnp.float32)
    if shards:
        drawn = drawn * levels(stream_key, extent, shards, -0.22, 0.18)
    return jnp.clip(drawn, -limit, limit).astype(kind)


def setup_inputs(seed: int = 0) -> dict:
    splits = jax.random.split(jax.random.key(seed), 5)
    cotangent = gaussian(splits[0], (SLOTS + 1, NX, NY, NZ), 1.0, 6.0, ((1, 8), (2, 4)), jnp.float32)
    fields_one = jnp.clip(1.0 * jax.random.uniform(splits[1], (SLOTS + 1, NX, NY, NZ), jnp.float32) ** levels(splits[1], (SLOTS + 1, NX, NY, NZ), ((1, 8), (2, 4)), -0.2, 0.2), 0.0, 1.0)
    fields_zero = jnp.clip(1.0 * jax.random.uniform(splits[2], (SLOTS + 1, NX, NY, NZ), jnp.float32) ** levels(splits[2], (SLOTS + 1, NX, NY, NZ), ((1, 8), (2, 4)), -0.2, 0.2), 0.0, 1.0)
    slot_grain = draw_slot_grain(jax.random.fold_in(splits[4], 71), 0)
    return {"cotangent": cotangent, "fields_one": fields_one, "fields_zero": fields_zero, "slot_grain": slot_grain}


time_step = 0.05
well_height = 16.0
barrier = 1.0


def laplace(value):
    extended = jnp.pad(value, [(0, 0)] * (value.ndim - 3) + [(1, 1)] * 3)
    total = extended[..., 2:, 1:-1, 1:-1] + extended[..., :-2, 1:-1, 1:-1]
    total = total + extended[..., 1:-1, 2:, 1:-1] + extended[..., 1:-1, :-2, 1:-1]
    total = total + extended[..., 1:-1, 1:-1, 2:] + extended[..., 1:-1, 1:-1, :-2]
    return total - 6.0 * value


def pointwise(costate, fields, lap_costate, lam_mu, lap_mu):
    density = fields[0]
    phases = fields[1:]
    lam_c = costate[0]
    lam_e = costate[1:]
    square_sum = jnp.sum(phases * phases, axis=0)
    weighted = jnp.sum(lam_e * phases, axis=0)
    coupled = jnp.sum(lam_e * (phases * phases - phases), axis=0)
    curvature = well_height * (2.0 - 12.0 * density + 12.0 * density * density) + 2.0 * barrier
    new_density = lam_c + lam_mu * curvature - lap_mu - 12.0 * barrier * time_step * coupled
    inner = lam_e * ((1.0 - density) - 2.0 * (2.0 - density) * phases + square_sum) + 2.0 * phases * weighted
    new_phases = lam_e - 12.0 * barrier * time_step * inner + time_step * lap_costate[1:]
    new_phases = new_phases + 12.0 * barrier * lam_mu * (phases * phases - phases)
    return jnp.concatenate([new_density[None], new_phases], axis=0)


def adjoint_step(costate, fields):
    lap_costate = laplace(costate)
    lam_mu = time_step * lap_costate[0]
    lap_mu = laplace(lam_mu)
    return pointwise(costate, fields, lap_costate, lam_mu, lap_mu)


def tile_rows(phase_costate):
    slots, size_x, size_y, depth = phase_costate.shape
    blocks = phase_costate.reshape(slots, size_x // TILE, TILE, size_y // TILE, TILE, depth)
    summed = jnp.sum(blocks, axis=(2, 4))
    return jnp.transpose(summed, (1, 2, 0, 3)).reshape(-1, depth)


def reference(cotangent, fields_one, fields_zero, slot_grain):
    costate_one = adjoint_step(cotangent, fields_one)
    adjoint_fields = adjoint_step(costate_one, fields_zero)
    partial_value = time_step * tile_rows(cotangent[1:]) + time_step * tile_rows(costate_one[1:])
    grain_grad = jax.ops.segment_sum(partial_value, slot_grain.reshape(-1).astype(jnp.int32), num_segments=GRAINS)
    return adjoint_fields, grain_grad
```

```python
import functools

import jax
import jax.numpy as jnp
from jax import lax
from jax.experimental import pallas as pl
from jax.experimental.pallas import tpu as pltpu
from jax.sharding import PartitionSpec as P

TILE = 8
GRAIN_DEV = 8
DT = 0.05
MESH = pl.DeviceIdType.MESH
LM = 9


def kernel(
    n_gx, n_gy, cot, f1, f0, slot_grain, out, grad,
    cp, c1p, lmp, f1v, f0v, ov, s1, w1, k1, s0, w2, k2, yh, ys, part, gsend, grecv,
    send_sem, recv_sem, load_sem, store_sem, gsend_sem, grecv_sem,
):
    fields, cx, cy, nz = cot.shape
    slots = fields - 1
    gx, gy = lax.axis_index("gx"), lax.axis_index("gy")
    can_send = (gx < n_gx - 1, gx > 0, gy < n_gy - 1, gy > 0)
    can_recv = (gx > 0, gx < n_gx - 1, gy > 0, gy < n_gy - 1)
    target = (
        (jnp.minimum(gx + 1, n_gx - 1), gy),
        (jnp.maximum(gx - 1, 0), gy),
        (gx, jnp.minimum(gy + 1, n_gy - 1)),
        (gx, jnp.maximum(gy - 1, 0)),
    )

    def load(source, dest, index):
        return pltpu.make_async_copy(source, dest, load_sem.at[index])

    loads = [load(cot.at[k], cp.at[k, pl.ds(1, cx)], k) for k in range(fields)]
    load_f1, load_f0 = load(f1, f1v, fields), load(f0, f0v, fields + 1)
    for copy in loads:
        copy.start()
    load_f1.start()
    load_f0.start()

    def remote(step, k, side):
        if side < 2:
            padded = lmp.at[step] if k == LM else (c1p.at[k] if step else cp.at[k])
            dst = padded.at[0 if side == 0 else cx + 1]
            edge = cx - 1 if side == 0 else 0
            if step == 0 and k != LM:
                src = cot.at[k, edge]
            else:
                src = padded.at[edge + 1]
        else:
            src, dst = ys.at[step, k, side - 2], yh.at[step, k, side - 2]
        return pltpu.make_async_remote_copy(
            src_ref=src, dst_ref=dst, send_sem=send_sem.at[step, k, side],
            recv_sem=recv_sem.at[step, k, side], device_id=target[side], device_id_type=MESH,
        )

    def send(step, k, sides=(0, 1, 2, 3)):
        for side in sides:
            pl.when(can_send[side])(lambda side=side: remote(step, k, side).start())

    def sent(step, k):
        for side in range(4):
            pl.when(can_send[side])(lambda side=side: remote(step, k, side).wait_send())

    def recv(step, k):
        for side in range(4):
            pl.when(can_recv[side])(lambda side=side: remote(step, k, side).wait_recv())

    def clear_x(row):
        zero = jnp.zeros((cy, nz), jnp.float32)

        def body(k, _):
            cp[k, row] = zero
            c1p[k, row] = zero
            return 0

        lax.fori_loop(0, fields, body, 0)
        lmp[0, row] = zero
        lmp[1, row] = zero

    def clear_y(side):
        zero = jnp.zeros((cx, nz), jnp.float32)

        def body(k, _):
            yh[0, k, side] = zero
            yh[1, k, side] = zero
            return 0

        lax.fori_loop(0, fields + 1, body, 0)

    pl.when(gx == 0)(lambda: clear_x(0))
    pl.when(gx == n_gx - 1)(lambda: clear_x(cx + 1))
    pl.when(gy == 0)(lambda: clear_y(0))
    pl.when(gy == n_gy - 1)(lambda: clear_y(1))

    barrier = pltpu.get_barrier_semaphore()
    for d in range(1, n_gx):
        pl.semaphore_signal(barrier, inc=1, device_id=(lax.rem(gx + d, n_gx), gy), device_id_type=MESH)
    for side in (2, 3):
        def greet(side=side):
            pl.semaphore_signal(barrier, inc=1, device_id=target[side], device_id_type=MESH)
        pl.when(can_send[side])(greet)
    beside = (gy > 0).astype(jnp.int32) + (gy < n_gy - 1).astype(jnp.int32)
    pl.semaphore_wait(barrier, n_gx - 1 + beside)

    for k in range(3):
        send(0, k, (0, 1))

    row_id = lax.broadcasted_iota(jnp.int32, (cy, nz), 0)
    lane_id = lax.broadcasted_iota(jnp.int32, (cy, nz), 1)

    def lap(ref, low, high, x):
        v = ref[x + 1]
        total = ref[x] + ref[x + 2]
        total += jnp.where(row_id == 0, low[pl.ds(x, 1), :], pltpu.roll(v, 1, 0))
        total += jnp.where(row_id == cy - 1, high[pl.ds(x, 1), :], pltpu.roll(v, cy - 1, 0))
        total += jnp.where(lane_id == 0, 0.0, pltpu.roll(v, 1, 1))
        total += jnp.where(lane_id == nz - 1, 0.0, pltpu.roll(v, nz - 1, 1))
        return v, total - 6.0 * v

    def stage(step, k, x, v):
        ys[step, k, 0, pl.ds(x, 1), :] = v[cy - 1 : cy]
        ys[step, k, 1, pl.ds(x, 1), :] = v[0:1]

    def over_x(body, init=0):
        return lax.fori_loop(0, cx, body, init)

    def stage_cot(k):
        loads[k].wait()

        def body(x, _):
            stage(0, k, x, cp[k, x + 1])
            return 0

        over_x(body)
        send(0, k, (2, 3))

    for k in range(fields):
        stage_cot(k)

    def potential(step):
        ref = c1p if step else cp

        def body(x, _):
            _, value = lap(ref.at[0], yh.at[step, 0, 0], yh.at[step, 0, 1], x)
            value = DT * value
            lmp[step, x + 1] = value
            stage(step, LM, x, value)
            return 0

        over_x(body)

    def density(step):
        ref, field, coupled = (c1p, f0v, k2) if step else (cp, f1v, k1)

        def body(x, _):
            lam_mu, lap_mu = lap(lmp.at[step], yh.at[step, LM, 0], yh.at[step, LM, 1], x)
            c = field[0, x]
            curvature = 16.0 * (2.0 - 12.0 * c + 12.0 * c * c) + 2.0
            value = ref[0, x + 1] + lam_mu * curvature - lap_mu - (12.0 * DT) * coupled[x]
            if step:
                ov[0, x] = value
            else:
                c1p[0, x + 1] = value
                stage(1, 0, x, value)
            return 0

        over_x(body)

    def phase(step, s):
        ref, field, base, weighted = (c1p, f0v, s0, w2) if step else (cp, f1v, s1, w1)

        def body(x, total):
            v, lap_v = lap(ref.at[s], yh.at[step, s, 0], yh.at[step, s, 1], x)
            eta, c = field[s, x], field[0, x]
            inner = v * (base[x] - 2.0 * (2.0 - c) * eta) + 2.0 * eta * weighted[x]
            value = v - (12.0 * DT) * inner + DT * lap_v
            value += 12.0 * lmp[step, x + 1] * (eta * eta - eta)
            if step:
                ov[s, x] = value
                return total
            c1p[s, x + 1] = value
            stage(1, s, x, value)
            old = f0v[s, x]
            first, second = value * old, value * (old * old - old)
            w2[x] = first if s == 1 else w2[x] + first
            k2[x] = second if s == 1 else k2[x] + second
            return total + (v + value)

        if step:
            over_x(body)
        else:
            total = over_x(body, jnp.zeros((cy, nz), jnp.float32))
            rows = jnp.sum(total.reshape(cy // TILE, TILE, nz), axis=1)
            part[pl.ds((s - 1) * (cy // TILE), cy // TILE), :] = DT * rows

    def store(k):
        return pltpu.make_async_copy(ov.at[k], out.at[k], store_sem.at[k])

    load_f1.wait()
    load_f0.wait()

    def sums(x, _):
        zero = jnp.zeros((cy, nz), jnp.float32)

        def body(s, carry):
            square, square_old, weighted, coupled = carry
            eta, old, lam = f1v[s, x], f0v[s, x], cp[s, x + 1]
            product = lam * eta
            eta_square = eta * eta
            return (square + eta_square, square_old + old * old, weighted + product, coupled + lam * (eta_square - eta))

        square, square_old, weighted, coupled = lax.fori_loop(1, fields, body, (zero, zero, zero, zero))
        s1[x] = (1.0 - f1v[0, x]) + square
        s0[x] = (1.0 - f0v[0, x]) + square_old
        w1[x] = weighted
        k1[x] = coupled
        return 0

    def grain_exchange(d):
        peer = lax.rem(gx + d, n_gx)
        return pltpu.make_async_remote_copy(
            src_ref=gsend.at[peer], dst_ref=grecv.at[d],
            send_sem=gsend_sem.at[d], recv_sem=grecv_sem.at[d],
            device_id=(peer, gy), device_id_type=MESH,
        )

    def grains():
        grain = slot_grain[...]
        owner = lax.div(lax.div(grain, GRAIN_DEV), n_gy)
        key = owner * GRAIN_DEV + lax.rem(grain, GRAIN_DEV)
        tiles = key.shape[0]
        column = lax.broadcasted_iota(jnp.int32, (tiles, n_gx * GRAIN_DEV), 1)
        chosen = jnp.concatenate(
            [(column == key[:, s : s + 1]).astype(jnp.float32) for s in range(slots)], axis=0
        )
        summed = lax.dot_general(
            chosen, part[...], (((0,), (0,)), ((), ())),
            precision=lax.Precision.HIGHEST, preferred_element_type=jnp.float32,
        )
        gsend[...] = summed.reshape(n_gx, GRAIN_DEV, nz)
        for d in range(1, n_gx):
            grain_exchange(d).start()

    recv(0, 0)
    potential(0)
    send(0, LM)
    send(0, 3, (0, 1))
    over_x(sums)

    def first(s):
        recv(0, s)
        phase(0, s)

    first(1)
    send(0, 4, (0, 1))
    first(2)
    recv(0, LM)
    density(0)
    send(1, 0)
    send(0, 5, (0, 1))
    first(3)
    send(0, 6, (0, 1))
    first(4)
    recv(1, 0)
    potential(1)
    send(1, LM)
    send(0, 7, (0, 1))
    first(5)
    send(0, 8, (0, 1))
    first(6)
    send(1, 1)
    recv(1, LM)
    send(1, 2)
    first(7)
    send(1, 3)
    first(8)
    send(1, 4)
    grains()
    density(1)
    store(0).start()
    for s in range(1, fields):
        recv(1, s)
        if s + 4 < fields:
            send(1, s + 4)
        phase(1, s)
        store(s).start()

    total = gsend[gx]
    for d in range(1, n_gx):
        grain_exchange(d).wait_recv()
        total += grecv[d]
    grad[...] = total
    for d in range(1, n_gx):
        grain_exchange(d).wait_send()
    for step in range(2):
        for k in range(fields + 1):
            sent(step, k)
    for k in range(fields):
        store(k).wait()


def solution(mesh):
    n_gx, n_gy = mesh.shape["gx"], mesh.shape["gy"]

    def shards(cotangent, fields_one, fields_zero, slot_grain):
        fields, cx, cy, nz = cotangent.shape
        whole = pltpu.VMEM((fields, cx, cy, nz), jnp.float32)
        padded = pltpu.VMEM((fields, cx + 2, cy, nz), jnp.float32)
        single = pltpu.VMEM((cx, cy, nz), jnp.float32)
        rows = pltpu.VMEM((2, fields + 1, 2, cx, nz), jnp.float32)
        tiles = cx // TILE * (cy // TILE)
        row_count = tiles * slot_grain.shape[-1]
        anywhere = pl.BlockSpec(memory_space=pl.ANY)
        vmem = pl.BlockSpec(memory_space=pltpu.VMEM)
        return pl.pallas_call(
            functools.partial(kernel, n_gx, n_gy),
            out_shape=(
                jax.ShapeDtypeStruct(cotangent.shape, jnp.float32),
                jax.ShapeDtypeStruct((GRAIN_DEV, nz), jnp.float32),
            ),
            in_specs=[anywhere, anywhere, anywhere, vmem],
            out_specs=(anywhere, vmem),
            scratch_shapes=[
                padded, padded, pltpu.VMEM((2, cx + 2, cy, nz), jnp.float32),
                whole, whole, whole,
                single, single, single, single, single, single,
                rows, rows,
                pltpu.VMEM((row_count, nz), jnp.float32),
                pltpu.VMEM((n_gx, GRAIN_DEV, nz), jnp.float32),
                pltpu.VMEM((n_gx, GRAIN_DEV, nz), jnp.float32),
                pltpu.SemaphoreType.DMA((2, fields + 1, 4)),
                pltpu.SemaphoreType.DMA((2, fields + 1, 4)),
                pltpu.SemaphoreType.DMA((fields + 2,)),
                pltpu.SemaphoreType.DMA((fields,)),
                pltpu.SemaphoreType.DMA((n_gx,)),
                pltpu.SemaphoreType.DMA((n_gx,)),
            ],
            compiler_params=pltpu.CompilerParams(
                collective_id=0, has_side_effects=True, vmem_limit_bytes=56 * 1024 * 1024
            ),
            cost_estimate=pl.CostEstimate(
                flops=100 * cotangent.size, bytes_accessed=16 * cotangent.size, transcendentals=0
            ),
        )(cotangent, fields_one, fields_zero, slot_grain.reshape(tiles, -1))

    placed = (
        P(None, "gx", "gy", None),
        P(None, "gx", "gy", None),
        P(None, "gx", "gy", None),
        P("gx", "gy", None),
    )
    return jax.shard_map(
        shards,
        mesh=mesh,
        in_specs=placed,
        out_specs=(P(None, "gx", "gy", None), P(("gx", "gy"), None)),
        check_vma=False,
    )
```

```python
import functools

import jax
import jax.numpy as jnp
from jax import lax
from jax.experimental import pallas as pl
from jax.experimental.pallas import tpu as pltpu
from jax.sharding import PartitionSpec as P

TILE = 8
GRAIN_DEV = 8
DT = 0.05
MESH = pl.DeviceIdType.MESH
LM = 9


def kernel(
    n_gx, n_gy, cot, f1, f0, slot_grain, out, grad,
    cp, c1p, lmp, f1v, f0v, s1, w1, k1, s0, w2, k2, yh, ys, part, gsend, grecv,
    send_sem, recv_sem, load_sem, gsend_sem, grecv_sem,
):
    fields, cx, cy, nz = cot.shape
    slots = fields - 1
    gx, gy = lax.axis_index("gx"), lax.axis_index("gy")
    can_send = (gx < n_gx - 1, gx > 0, gy < n_gy - 1, gy > 0)
    can_recv = (gx > 0, gx < n_gx - 1, gy > 0, gy < n_gy - 1)
    target = (
        (jnp.minimum(gx + 1, n_gx - 1), gy),
        (jnp.maximum(gx - 1, 0), gy),
        (gx, jnp.minimum(gy + 1, n_gy - 1)),
        (gx, jnp.maximum(gy - 1, 0)),
    )

    def load(source, dest, index):
        return pltpu.make_async_copy(source, dest, load_sem.at[index])

    loads = [load(cot.at[k], cp.at[k, pl.ds(1, cx)], k) for k in range(fields)]
    load_f1, load_f0 = load(f1, f1v, fields), load(f0, f0v, fields + 1)
    for copy in loads:
        copy.start()
    load_f1.start()
    load_f0.start()

    def remote(step, k, side):
        if side < 2:
            padded = lmp.at[step] if k == LM else (c1p.at[k] if step else cp.at[k])
            dst = padded.at[0 if side == 0 else cx + 1]
            edge = cx - 1 if side == 0 else 0
            if step == 0 and k != LM:
                src = cot.at[k, edge]
            else:
                src = padded.at[edge + 1]
        else:
            src, dst = ys.at[step, k, side - 2], yh.at[step, k, side - 2]
        return pltpu.make_async_remote_copy(
            src_ref=src, dst_ref=dst, send_sem=send_sem.at[step, k, side],
            recv_sem=recv_sem.at[step, k, side], device_id=target[side], device_id_type=MESH,
        )

    def send(step, k, sides=(0, 1, 2, 3)):
        for side in sides:
            pl.when(can_send[side])(lambda side=side: remote(step, k, side).start())

    def sent(step, k):
        for side in range(4):
            pl.when(can_send[side])(lambda side=side: remote(step, k, side).wait_send())

    def recv(step, k):
        for side in range(4):
            pl.when(can_recv[side])(lambda side=side: remote(step, k, side).wait_recv())

    def clear_x(row):
        zero = jnp.zeros((cy, nz), jnp.float32)

        def body(k, _):
            cp[k, row] = zero
            c1p[k, row] = zero
            return 0

        lax.fori_loop(0, fields, body, 0)
        lmp[0, row] = zero
        lmp[1, row] = zero

    def clear_y(side):
        zero = jnp.zeros((cx, nz), jnp.float32)

        def body(k, _):
            yh[0, k, side] = zero
            yh[1, k, side] = zero
            return 0

        lax.fori_loop(0, fields + 1, body, 0)

    pl.when(gx == 0)(lambda: clear_x(0))
    pl.when(gx == n_gx - 1)(lambda: clear_x(cx + 1))
    pl.when(gy == 0)(lambda: clear_y(0))
    pl.when(gy == n_gy - 1)(lambda: clear_y(1))

    barrier = pltpu.get_barrier_semaphore()
    for d in range(1, n_gx):
        pl.semaphore_signal(barrier, inc=1, device_id=(lax.rem(gx + d, n_gx), gy), device_id_type=MESH)
    for side in (2, 3):
        def greet(side=side):
            pl.semaphore_signal(barrier, inc=1, device_id=target[side], device_id_type=MESH)
        pl.when(can_send[side])(greet)
    beside = (gy > 0).astype(jnp.int32) + (gy < n_gy - 1).astype(jnp.int32)
    pl.semaphore_wait(barrier, n_gx - 1 + beside)

    for k in range(5):
        send(0, k, (0, 1))

    row_id = lax.broadcasted_iota(jnp.int32, (cy, nz), 0)
    lane_id = lax.broadcasted_iota(jnp.int32, (cy, nz), 1)

    def lap(ref, low, high, x):
        v = ref[x + 1]
        total = ref[x] + ref[x + 2]
        total += jnp.where(row_id == 0, low[pl.ds(x, 1), :], pltpu.roll(v, 1, 0))
        total += jnp.where(row_id == cy - 1, high[pl.ds(x, 1), :], pltpu.roll(v, cy - 1, 0))
        total += jnp.where(lane_id == 0, 0.0, pltpu.roll(v, 1, 1))
        total += jnp.where(lane_id == nz - 1, 0.0, pltpu.roll(v, nz - 1, 1))
        return v, total - 6.0 * v

    def stage(step, k, x, v):
        ys[step, k, 0, pl.ds(x, 1), :] = v[cy - 1 : cy]
        ys[step, k, 1, pl.ds(x, 1), :] = v[0:1]

    def over_x(body, init=0):
        return lax.fori_loop(0, cx, body, init)

    def stage_cot(k):
        loads[k].wait()

        def body(x, _):
            stage(0, k, x, cp[k, x + 1])
            return 0

        over_x(body)
        send(0, k, (2, 3))

    for k in range(fields):
        stage_cot(k)

    def potential(step):
        ref = c1p if step else cp

        def body(x, _):
            _, value = lap(ref.at[0], yh.at[step, 0, 0], yh.at[step, 0, 1], x)
            value = DT * value
            lmp[step, x + 1] = value
            stage(step, LM, x, value)
            return 0

        over_x(body)

    def density(step):
        ref, field, coupled = (c1p, f0v, k2) if step else (cp, f1v, k1)

        def body(x, _):
            lam_mu, lap_mu = lap(lmp.at[step], yh.at[step, LM, 0], yh.at[step, LM, 1], x)
            c = field[0, x]
            curvature = 16.0 * (2.0 - 12.0 * c + 12.0 * c * c) + 2.0
            value = ref[0, x + 1] + lam_mu * curvature - lap_mu - (12.0 * DT) * coupled[x]
            if step:
                out[0, x] = value
            else:
                c1p[0, x + 1] = value
                stage(1, 0, x, value)
            return 0

        over_x(body)

    def phase(step, s):
        ref, field, base, weighted = (c1p, f0v, s0, w2) if step else (cp, f1v, s1, w1)

        def body(x, total):
            v, lap_v = lap(ref.at[s], yh.at[step, s, 0], yh.at[step, s, 1], x)
            eta, c = field[s, x], field[0, x]
            inner = v * (base[x] - 2.0 * (2.0 - c) * eta) + 2.0 * eta * weighted[x]
            value = v - (12.0 * DT) * inner + DT * lap_v
            value += 12.0 * lmp[step, x + 1] * (eta * eta - eta)
            if step:
                out[s, x] = value
                return total
            c1p[s, x + 1] = value
            stage(1, s, x, value)
            old = f0v[s, x]
            first, second = value * old, value * (old * old - old)
            w2[x] = first if s == 1 else w2[x] + first
            k2[x] = second if s == 1 else k2[x] + second
            return total + (v + value)

        if step:
            over_x(body)
        else:
            total = over_x(body, jnp.zeros((cy, nz), jnp.float32))
            rows = jnp.sum(total.reshape(cy // TILE, TILE, nz), axis=1)
            part[pl.ds((s - 1) * (cy // TILE), cy // TILE), :] = DT * rows

    load_f1.wait()
    load_f0.wait()

    def sums(x, _):
        zero = jnp.zeros((cy, nz), jnp.float32)

        def body(s, carry):
            square, square_old, weighted, coupled = carry
            eta, old, lam = f1v[s, x], f0v[s, x], cp[s, x + 1]
            product = lam * eta
            eta_square = eta * eta
            return (square + eta_square, square_old + old * old, weighted + product, coupled + lam * (eta_square - eta))

        square, square_old, weighted, coupled = lax.fori_loop(1, fields, body, (zero, zero, zero, zero))
        s1[x] = (1.0 - f1v[0, x]) + square
        s0[x] = (1.0 - f0v[0, x]) + square_old
        w1[x] = weighted
        k1[x] = coupled
        return 0

    def grain_exchange(d):
        peer = lax.rem(gx + d, n_gx)
        return pltpu.make_async_remote_copy(
            src_ref=gsend.at[peer], dst_ref=grecv.at[d],
            send_sem=gsend_sem.at[d], recv_sem=grecv_sem.at[d],
            device_id=(peer, gy), device_id_type=MESH,
        )

    def grains():
        grain = slot_grain[...]
        owner = lax.div(lax.div(grain, GRAIN_DEV), n_gy)
        key = owner * GRAIN_DEV + lax.rem(grain, GRAIN_DEV)
        tiles = key.shape[0]
        column = lax.broadcasted_iota(jnp.int32, (tiles, n_gx * GRAIN_DEV), 1)
        chosen = jnp.concatenate(
            [(column == key[:, s : s + 1]).astype(jnp.float32) for s in range(slots)], axis=0
        )
        summed = lax.dot_general(
            chosen, part[...], (((0,), (0,)), ((), ())),
            precision=lax.Precision.HIGHEST, preferred_element_type=jnp.float32,
        )
        gsend[...] = summed.reshape(n_gx, GRAIN_DEV, nz)
        for d in range(1, n_gx):
            grain_exchange(d).start()

    recv(0, 0)
    potential(0)
    send(0, LM)
    send(0, 5, (0, 1))
    over_x(sums)

    def first(s):
        recv(0, s)
        phase(0, s)

    for s in (1, 2, 3):
        first(s)
        send(0, s + 5, (0, 1))
    first(4)
    send(1, 1)
    recv(0, LM)
    density(0)
    send(1, 0)
    for s in (5, 6, 7, 8):
        first(s)
        send(1, s - 3)
    recv(1, 0)
    potential(1)
    send(1, LM)
    send(1, 6)
    grains()

    def second(s):
        recv(1, s)
        phase(1, s)

    second(1)
    send(1, 7)
    second(2)
    send(1, 8)
    second(3)
    second(4)
    recv(1, LM)
    density(1)
    for s in (5, 6, 7, 8):
        second(s)

    total = gsend[gx]
    for d in range(1, n_gx):
        grain_exchange(d).wait_recv()
        total += grecv[d]
    grad[...] = total
    for d in range(1, n_gx):
        grain_exchange(d).wait_send()
    for step in range(2):
        for k in range(fields + 1):
            sent(step, k)


def solution(mesh):
    n_gx, n_gy = mesh.shape["gx"], mesh.shape["gy"]

    def shards(cotangent, fields_one, fields_zero, slot_grain):
        fields, cx, cy, nz = cotangent.shape
        whole = pltpu.VMEM((fields, cx, cy, nz), jnp.float32)
        padded = pltpu.VMEM((fields, cx + 2, cy, nz), jnp.float32)
        single = pltpu.VMEM((cx, cy, nz), jnp.float32)
        rows = pltpu.VMEM((2, fields + 1, 2, cx, nz), jnp.float32)
        tiles = cx // TILE * (cy // TILE)
        row_count = tiles * slot_grain.shape[-1]
        far = pl.BlockSpec(memory_space=pltpu.HBM)
        vmem = pl.BlockSpec(memory_space=pltpu.VMEM)
        return pl.pallas_call(
            functools.partial(kernel, n_gx, n_gy),
            out_shape=(
                pltpu.VMEM(cotangent.shape, jnp.float32),
                jax.ShapeDtypeStruct((GRAIN_DEV, nz), jnp.float32),
            ),
            in_specs=[far, far, far, vmem],
            out_specs=(vmem, vmem),
            scratch_shapes=[
                padded, padded, pltpu.VMEM((2, cx + 2, cy, nz), jnp.float32),
                whole, whole,
                single, single, single, single, single, single,
                rows, rows,
                pltpu.VMEM((row_count, nz), jnp.float32),
                pltpu.VMEM((n_gx, GRAIN_DEV, nz), jnp.float32),
                pltpu.VMEM((n_gx, GRAIN_DEV, nz), jnp.float32),
                pltpu.SemaphoreType.DMA((2, fields + 1, 4)),
                pltpu.SemaphoreType.DMA((2, fields + 1, 4)),
                pltpu.SemaphoreType.DMA((fields + 2,)),
                pltpu.SemaphoreType.DMA((n_gx,)),
                pltpu.SemaphoreType.DMA((n_gx,)),
            ],
            compiler_params=pltpu.CompilerParams(
                collective_id=0, has_side_effects=True, vmem_limit_bytes=48 * 1024 * 1024
            ),
            cost_estimate=pl.CostEstimate(
                flops=100 * cotangent.size, bytes_accessed=16 * cotangent.size, transcendentals=0
            ),
        )(cotangent, fields_one, fields_zero, slot_grain.reshape(tiles, -1))

    placed = (
        P(None, "gx", "gy", None),
        P(None, "gx", "gy", None),
        P(None, "gx", "gy", None),
        P("gx", "gy", None),
    )
    return jax.shard_map(
        shards,
        mesh=mesh,
        in_specs=placed,
        out_specs=(P(None, "gx", "gy", None), P(("gx", "gy"), None)),
        check_vma=False,
    )
```

```python
import functools

import jax
import jax.numpy as jnp
from jax import lax
from jax.experimental import pallas as pl
from jax.experimental.pallas import tpu as pltpu
from jax.sharding import PartitionSpec as P

TILE = 8
GRAIN_DEV = 8
DT = 0.05
MESH = pl.DeviceIdType.MESH
LM = 9


def kernel(
    n_gx, n_gy, cot, f1, f0, slot_grain, out, grad,
    cp, c1p, lmp, f1v, f0v, s1, w1, k1, s0, w2, k2, yh, ys, part, gv, gsend, grecv,
    send_sem, recv_sem, load_sem, gsend_sem, grecv_sem,
):
    fields, cx, cy, nz = cot.shape
    slots = fields - 1
    gx, gy = lax.axis_index("gx"), lax.axis_index("gy")
    can_send = (gx < n_gx - 1, gx > 0, gy < n_gy - 1, gy > 0)
    can_recv = (gx > 0, gx < n_gx - 1, gy > 0, gy < n_gy - 1)
    target = (
        (jnp.minimum(gx + 1, n_gx - 1), gy),
        (jnp.maximum(gx - 1, 0), gy),
        (gx, jnp.minimum(gy + 1, n_gy - 1)),
        (gx, jnp.maximum(gy - 1, 0)),
    )

    barrier = pltpu.get_barrier_semaphore()
    for d in range(1, n_gx):
        pl.semaphore_signal(barrier, inc=1, device_id=(lax.rem(gx + d, n_gx), gy), device_id_type=MESH)
    for side in (2, 3):
        def greet(side=side):
            pl.semaphore_signal(barrier, inc=1, device_id=target[side], device_id_type=MESH)
        pl.when(can_send[side])(greet)
    def load(source, dest, index):
        return pltpu.make_async_copy(source, dest, load_sem.at[index])

    loads = [load(cot.at[k], cp.at[k, pl.ds(1, cx)], k) for k in range(fields)]
    load_f1, load_f0 = load(f1, f1v, fields), load(f0, f0v, fields + 1)
    load_grain = load(slot_grain, gv, fields + 2)
    for copy in loads:
        copy.start()
    load_f1.start()
    load_f0.start()
    load_grain.start()

    def remote(step, k, side):
        if side < 2:
            padded = lmp.at[step] if k == LM else (c1p.at[k] if step else cp.at[k])
            dst = padded.at[0 if side == 0 else cx + 1]
            edge = cx - 1 if side == 0 else 0
            if step == 0 and k != LM:
                src = cot.at[k, edge]
            else:
                src = padded.at[edge + 1]
        else:
            src, dst = ys.at[step, k, side - 2], yh.at[step, k, side - 2]
        return pltpu.make_async_remote_copy(
            src_ref=src, dst_ref=dst, send_sem=send_sem.at[step, k, side],
            recv_sem=recv_sem.at[step, k, side], device_id=target[side], device_id_type=MESH,
        )

    def send(step, k, sides=(0, 1, 2, 3)):
        for side in sides:
            pl.when(can_send[side])(lambda side=side: remote(step, k, side).start())

    def sent(step, k):
        for side in range(4):
            pl.when(can_send[side])(lambda side=side: remote(step, k, side).wait_send())

    def recv(step, k):
        for side in range(4):
            pl.when(can_recv[side])(lambda side=side: remote(step, k, side).wait_recv())

    def clear_x(row):
        zero = jnp.zeros((cy, nz), jnp.float32)

        def body(k, _):
            cp[k, row] = zero
            c1p[k, row] = zero
            return 0

        lax.fori_loop(0, fields, body, 0)
        lmp[0, row] = zero
        lmp[1, row] = zero

    def clear_y(side):
        zero = jnp.zeros((cx, nz), jnp.float32)

        def body(k, _):
            yh[0, k, side] = zero
            yh[1, k, side] = zero
            return 0

        lax.fori_loop(0, fields + 1, body, 0)

    pl.when(gx == 0)(lambda: clear_x(0))
    pl.when(gx == n_gx - 1)(lambda: clear_x(cx + 1))
    pl.when(gy == 0)(lambda: clear_y(0))
    pl.when(gy == n_gy - 1)(lambda: clear_y(1))

    beside = (gy > 0).astype(jnp.int32) + (gy < n_gy - 1).astype(jnp.int32)
    pl.semaphore_wait(barrier, n_gx - 1 + beside)

    for k in range(5):
        send(0, k, (0, 1))

    row_id = lax.broadcasted_iota(jnp.int32, (cy, nz), 0)
    lane_id = lax.broadcasted_iota(jnp.int32, (cy, nz), 1)

    def lap(ref, low, high, x):
        v = ref[x + 1]
        total = ref[x] + ref[x + 2]
        total += jnp.where(row_id == 0, low[pl.ds(x, 1), :], pltpu.roll(v, 1, 0))
        total += jnp.where(row_id == cy - 1, high[pl.ds(x, 1), :], pltpu.roll(v, cy - 1, 0))
        total += jnp.where(lane_id == 0, 0.0, pltpu.roll(v, 1, 1))
        total += jnp.where(lane_id == nz - 1, 0.0, pltpu.roll(v, nz - 1, 1))
        return v, total - 6.0 * v

    def stage(step, k, x, v):
        ys[step, k, 0, pl.ds(x, 1), :] = v[cy - 1 : cy]
        ys[step, k, 1, pl.ds(x, 1), :] = v[0:1]

    def over_x(body, init=0):
        return lax.fori_loop(0, cx, body, init)

    def stage_cot(k):
        loads[k].wait()

        def body(x, _):
            stage(0, k, x, cp[k, x + 1])
            return 0

        over_x(body)
        send(0, k, (2, 3))

    for k in range(fields):
        stage_cot(k)

    def potential(step):
        ref = c1p if step else cp

        def body(x, _):
            _, value = lap(ref.at[0], yh.at[step, 0, 0], yh.at[step, 0, 1], x)
            value = DT * value
            lmp[step, x + 1] = value
            stage(step, LM, x, value)
            return 0

        over_x(body)

    def density(step):
        ref, field, coupled = (c1p, f0v, k2) if step else (cp, f1v, k1)

        def body(x, _):
            lam_mu, lap_mu = lap(lmp.at[step], yh.at[step, LM, 0], yh.at[step, LM, 1], x)
            c = field[0, x]
            curvature = 16.0 * (2.0 - 12.0 * c + 12.0 * c * c) + 2.0
            value = ref[0, x + 1] + lam_mu * curvature - lap_mu - (12.0 * DT) * coupled[x]
            if step:
                out[0, x] = value
            else:
                c1p[0, x + 1] = value
                stage(1, 0, x, value)
            return 0

        over_x(body)

    def phase(step, s):
        ref, field, base, weighted = (c1p, f0v, s0, w2) if step else (cp, f1v, s1, w1)

        def body(x, total):
            v, lap_v = lap(ref.at[s], yh.at[step, s, 0], yh.at[step, s, 1], x)
            eta, c = field[s, x], field[0, x]
            inner = v * (base[x] - 2.0 * (2.0 - c) * eta) + 2.0 * eta * weighted[x]
            value = v - (12.0 * DT) * inner + DT * lap_v
            value += 12.0 * lmp[step, x + 1] * (eta * eta - eta)
            if step:
                out[s, x] = value
                return total
            c1p[s, x + 1] = value
            stage(1, s, x, value)
            old = f0v[s, x]
            first, second = value * old, value * (old * old - old)
            w2[x] = first if s == 1 else w2[x] + first
            k2[x] = second if s == 1 else k2[x] + second
            return total + (v + value)

        if step:
            over_x(body)
        else:
            total = over_x(body, jnp.zeros((cy, nz), jnp.float32))
            rows = jnp.sum(total.reshape(cy // TILE, TILE, nz), axis=1)
            part[pl.ds((s - 1) * (cy // TILE), cy // TILE), :] = DT * rows

    load_f1.wait()
    load_f0.wait()

    def sums(x, _):
        zero = jnp.zeros((cy, nz), jnp.float32)

        def body(s, carry):
            square, square_old, weighted, coupled = carry
            eta, old, lam = f1v[s, x], f0v[s, x], cp[s, x + 1]
            product = lam * eta
            eta_square = eta * eta
            return (square + eta_square, square_old + old * old, weighted + product, coupled + lam * (eta_square - eta))

        square, square_old, weighted, coupled = lax.fori_loop(1, fields, body, (zero, zero, zero, zero))
        s1[x] = (1.0 - f1v[0, x]) + square
        s0[x] = (1.0 - f0v[0, x]) + square_old
        w1[x] = weighted
        k1[x] = coupled
        return 0

    def grain_exchange(d):
        peer = lax.rem(gx + d, n_gx)
        return pltpu.make_async_remote_copy(
            src_ref=gsend.at[peer], dst_ref=grecv.at[d],
            send_sem=gsend_sem.at[d], recv_sem=grecv_sem.at[d],
            device_id=(peer, gy), device_id_type=MESH,
        )

    def grains():
        load_grain.wait()
        grain = gv[...]
        owner = lax.div(lax.div(grain, GRAIN_DEV), n_gy)
        key = owner * GRAIN_DEV + lax.rem(grain, GRAIN_DEV)
        tiles = key.shape[0]
        column = lax.broadcasted_iota(jnp.int32, (tiles, n_gx * GRAIN_DEV), 1)
        chosen = jnp.concatenate(
            [(column == key[:, s : s + 1]).astype(jnp.float32) for s in range(slots)], axis=0
        )
        summed = lax.dot_general(
            chosen, part[...], (((0,), (0,)), ((), ())),
            precision=lax.Precision.HIGHEST, preferred_element_type=jnp.float32,
        )
        gsend[...] = summed.reshape(n_gx, GRAIN_DEV, nz)
        for d in range(1, n_gx):
            grain_exchange(d).start()

    recv(0, 0)
    potential(0)
    send(0, LM)
    send(0, 5, (0, 1))
    over_x(sums)

    def first(s):
        recv(0, s)
        phase(0, s)

    for s in (1, 2, 3):
        first(s)
        send(0, s + 5, (0, 1))
    first(4)
    send(1, 1)
    recv(0, LM)
    density(0)
    send(1, 0)
    for s in (5, 6, 7, 8):
        first(s)
        send(1, s - 3)
    recv(1, 0)
    potential(1)
    send(1, LM)
    send(1, 6)
    grains()

    def second(s):
        recv(1, s)
        phase(1, s)

    second(1)
    send(1, 7)
    second(2)
    send(1, 8)
    second(3)
    second(4)
    recv(1, LM)
    density(1)
    second(5)
    for k in range(fields + 1):
        sent(0, k)
    second(6)
    total = gsend[gx]
    for d in range(1, n_gx):
        grain_exchange(d).wait_recv()
        total += grecv[d]
    grad[...] = total
    for d in range(1, n_gx):
        grain_exchange(d).wait_send()
    second(7)
    for k in (0, 1, 2, 3, 4, 5, 6, LM):
        sent(1, k)
    second(8)
    sent(1, 7)
    sent(1, 8)


def solution(mesh):
    n_gx, n_gy = mesh.shape["gx"], mesh.shape["gy"]

    def shards(cotangent, fields_one, fields_zero, slot_grain):
        fields, cx, cy, nz = cotangent.shape
        whole = pltpu.VMEM((fields, cx, cy, nz), jnp.float32)
        padded = pltpu.VMEM((fields, cx + 2, cy, nz), jnp.float32)
        single = pltpu.VMEM((cx, cy, nz), jnp.float32)
        rows = pltpu.VMEM((2, fields + 1, 2, cx, nz), jnp.float32)
        tiles = cx // TILE * (cy // TILE)
        row_count = tiles * slot_grain.shape[-1]
        far = pl.BlockSpec(memory_space=pltpu.HBM)
        vmem = pl.BlockSpec(memory_space=pltpu.VMEM)
        return pl.pallas_call(
            functools.partial(kernel, n_gx, n_gy),
            out_shape=(
                pltpu.VMEM(cotangent.shape, jnp.float32),
                jax.ShapeDtypeStruct((GRAIN_DEV, nz), jnp.float32),
            ),
            in_specs=[far, far, far, far],
            out_specs=(vmem, vmem),
            scratch_shapes=[
                padded, padded, pltpu.VMEM((2, cx + 2, cy, nz), jnp.float32),
                whole, whole,
                single, single, single, single, single, single,
                rows, rows,
                pltpu.VMEM((row_count, nz), jnp.float32),
                pltpu.VMEM((tiles, slot_grain.shape[-1]), jnp.int32),
                pltpu.VMEM((n_gx, GRAIN_DEV, nz), jnp.float32),
                pltpu.VMEM((n_gx, GRAIN_DEV, nz), jnp.float32),
                pltpu.SemaphoreType.DMA((2, fields + 1, 4)),
                pltpu.SemaphoreType.DMA((2, fields + 1, 4)),
                pltpu.SemaphoreType.DMA((fields + 3,)),
                pltpu.SemaphoreType.DMA((n_gx,)),
                pltpu.SemaphoreType.DMA((n_gx,)),
            ],
            compiler_params=pltpu.CompilerParams(
                collective_id=0, has_side_effects=True, vmem_limit_bytes=48 * 1024 * 1024
            ),
            cost_estimate=pl.CostEstimate(
                flops=100 * cotangent.size, bytes_accessed=16 * cotangent.size, transcendentals=0
            ),
        )(cotangent, fields_one, fields_zero, slot_grain.reshape(tiles, -1))

    placed = (
        P(None, "gx", "gy", None),
        P(None, "gx", "gy", None),
        P(None, "gx", "gy", None),
        P("gx", "gy", None),
    )
    return jax.shard_map(
        shards,
        mesh=mesh,
        in_specs=placed,
        out_specs=(P(None, "gx", "gy", None), P(("gx", "gy"), None)),
        check_vma=False,
    )
```

```python
import functools

import jax
import jax.numpy as jnp
from jax import lax
from jax.experimental import pallas as pl
from jax.experimental.pallas import tpu as pltpu
from jax.sharding import PartitionSpec as P

TILE = 8
GRAIN_DEV = 8
DT = 0.05
MESH = pl.DeviceIdType.MESH
LM = 9


def kernel(
    n_gx, n_gy, cot, f1, f0, slot_grain, out, grad,
    cp, c1p, lmp, f1v, f0v, s1, w1, k1, s0, w2, k2, yh, ys, part, gv, gsend, grecv,
    send_sem, recv_sem, load_sem, gsend_sem, grecv_sem,
):
    fields, cx, cy, nz = cot.shape
    slots = fields - 1
    gx, gy = lax.axis_index("gx"), lax.axis_index("gy")
    can_send = (gx < n_gx - 1, gx > 0, gy < n_gy - 1, gy > 0)
    can_recv = (gx > 0, gx < n_gx - 1, gy > 0, gy < n_gy - 1)
    target = (
        (jnp.minimum(gx + 1, n_gx - 1), gy),
        (jnp.maximum(gx - 1, 0), gy),
        (gx, jnp.minimum(gy + 1, n_gy - 1)),
        (gx, jnp.maximum(gy - 1, 0)),
    )

    barrier = pltpu.get_barrier_semaphore()
    for d in range(1, n_gx):
        pl.semaphore_signal(barrier, inc=1, device_id=(lax.rem(gx + d, n_gx), gy), device_id_type=MESH)
    for side in (2, 3):
        def greet(side=side):
            pl.semaphore_signal(barrier, inc=1, device_id=target[side], device_id_type=MESH)
        pl.when(can_send[side])(greet)
    def load(source, dest, index):
        return pltpu.make_async_copy(source, dest, load_sem.at[index])

    loads = [load(cot.at[k], cp.at[k, pl.ds(1, cx)], k) for k in range(fields)]
    load_f1, load_f0 = load(f1, f1v, fields), load(f0, f0v, fields + 1)
    load_grain = load(slot_grain, gv, fields + 2)
    for copy in loads:
        copy.start()
    load_f1.start()
    load_f0.start()
    load_grain.start()

    def remote(step, k, side):
        if side < 2:
            padded = lmp.at[step] if k == LM else (c1p.at[k] if step else cp.at[k])
            dst = padded.at[0 if side == 0 else cx + 1]
            edge = cx - 1 if side == 0 else 0
            if step == 0 and k != LM:
                src = cot.at[k, edge]
            else:
                src = padded.at[edge + 1]
        else:
            src, dst = ys.at[step, k, side - 2], yh.at[step, k, side - 2]
        return pltpu.make_async_remote_copy(
            src_ref=src, dst_ref=dst, send_sem=send_sem.at[step, k, side],
            recv_sem=recv_sem.at[step, k, side], device_id=target[side], device_id_type=MESH,
        )

    def send(step, k, sides=(0, 1, 2, 3)):
        for side in sides:
            pl.when(can_send[side])(lambda side=side: remote(step, k, side).start())

    def sent(step, k):
        for side in range(4):
            pl.when(can_send[side])(lambda side=side: remote(step, k, side).wait_send())

    def recv(step, k):
        for side in range(4):
            pl.when(can_recv[side])(lambda side=side: remote(step, k, side).wait_recv())

    def clear_x(row):
        zero = jnp.zeros((cy, nz), jnp.float32)

        def body(k, _):
            cp[k, row] = zero
            c1p[k, row] = zero
            return 0

        lax.fori_loop(0, fields, body, 0)
        lmp[0, row] = zero
        lmp[1, row] = zero

    def clear_y(side):
        zero = jnp.zeros((cx, nz), jnp.float32)

        def body(k, _):
            yh[0, k, side] = zero
            yh[1, k, side] = zero
            return 0

        lax.fori_loop(0, fields + 1, body, 0)

    pl.when(gx == 0)(lambda: clear_x(0))
    pl.when(gx == n_gx - 1)(lambda: clear_x(cx + 1))
    pl.when(gy == 0)(lambda: clear_y(0))
    pl.when(gy == n_gy - 1)(lambda: clear_y(1))

    beside = (gy > 0).astype(jnp.int32) + (gy < n_gy - 1).astype(jnp.int32)
    pl.semaphore_wait(barrier, n_gx - 1 + beside)

    for k in range(5):
        send(0, k, (0, 1))

    row_id = lax.broadcasted_iota(jnp.int32, (cy, nz), 0)
    lane_id = lax.broadcasted_iota(jnp.int32, (cy, nz), 1)

    def lap(ref, low, high, x):
        v = ref[x + 1]
        total = ref[x] + ref[x + 2]
        total += jnp.where(row_id == 0, low[pl.ds(x, 1), :], pltpu.roll(v, 1, 0))
        total += jnp.where(row_id == cy - 1, high[pl.ds(x, 1), :], pltpu.roll(v, cy - 1, 0))
        total += jnp.where(lane_id == 0, 0.0, pltpu.roll(v, 1, 1))
        total += jnp.where(lane_id == nz - 1, 0.0, pltpu.roll(v, nz - 1, 1))
        return v, total - 6.0 * v

    def stage(step, k, x, v):
        ys[step, k, 0, pl.ds(x, 1), :] = v[cy - 1 : cy]
        ys[step, k, 1, pl.ds(x, 1), :] = v[0:1]

    def over_x(body, init=0):
        return lax.fori_loop(0, cx, body, init)

    def stage_cot(k):
        loads[k].wait()

        def body(x, _):
            stage(0, k, x, cp[k, x + 1])
            return 0

        over_x(body)
        send(0, k, (2, 3))

    for k in range(fields):
        stage_cot(k)

    def potential(step):
        ref = c1p if step else cp

        def body(x, _):
            _, value = lap(ref.at[0], yh.at[step, 0, 0], yh.at[step, 0, 1], x)
            value = DT * value
            lmp[step, x + 1] = value
            stage(step, LM, x, value)
            return 0

        over_x(body)

    def density(step):
        ref, field, coupled = (c1p, f0v, k2) if step else (cp, f1v, k1)

        def body(x, _):
            lam_mu, lap_mu = lap(lmp.at[step], yh.at[step, LM, 0], yh.at[step, LM, 1], x)
            c = field[0, x]
            curvature = 16.0 * (2.0 - 12.0 * c + 12.0 * c * c) + 2.0
            value = ref[0, x + 1] + lam_mu * curvature - lap_mu - (12.0 * DT) * coupled[x]
            if step:
                out[0, x] = value
            else:
                c1p[0, x + 1] = value
                stage(1, 0, x, value)
            return 0

        over_x(body)

    def phase(step, s):
        ref, field, base, weighted = (c1p, f0v, s0, w2) if step else (cp, f1v, s1, w1)

        def body(x, total):
            v, lap_v = lap(ref.at[s], yh.at[step, s, 0], yh.at[step, s, 1], x)
            eta, c = field[s, x], field[0, x]
            inner = v * (base[x] - 2.0 * (2.0 - c) * eta) + 2.0 * eta * weighted[x]
            value = v - (12.0 * DT) * inner + DT * lap_v
            value += 12.0 * lmp[step, x + 1] * (eta * eta - eta)
            if step:
                out[s, x] = value
                return total
            c1p[s, x + 1] = value
            stage(1, s, x, value)
            old = f0v[s, x]
            first, second = value * old, value * (old * old - old)
            w2[x] = first if s == 1 else w2[x] + first
            k2[x] = second if s == 1 else k2[x] + second
            return total + (v + value)

        if step:
            over_x(body)
        else:
            total = over_x(body, jnp.zeros((cy, nz), jnp.float32))
            rows = jnp.sum(total.reshape(cy // TILE, TILE, nz), axis=1)
            part[pl.ds((s - 1) * (cy // TILE), cy // TILE), :] = DT * rows

    load_f1.wait()
    load_f0.wait()

    def sums(x, _):
        zero = jnp.zeros((cy, nz), jnp.float32)

        def body(s, carry):
            square, square_old, weighted, coupled = carry
            eta, old, lam = f1v[s, x], f0v[s, x], cp[s, x + 1]
            product = lam * eta
            eta_square = eta * eta
            return (square + eta_square, square_old + old * old, weighted + product, coupled + lam * (eta_square - eta))

        square, square_old, weighted, coupled = lax.fori_loop(1, fields, body, (zero, zero, zero, zero))
        s1[x] = (1.0 - f1v[0, x]) + square
        s0[x] = (1.0 - f0v[0, x]) + square_old
        w1[x] = weighted
        k1[x] = coupled
        return 0

    def grain_exchange(d):
        peer = lax.rem(gx + d, n_gx)
        return pltpu.make_async_remote_copy(
            src_ref=gsend.at[peer], dst_ref=grecv.at[d],
            send_sem=gsend_sem.at[d], recv_sem=grecv_sem.at[d],
            device_id=(peer, gy), device_id_type=MESH,
        )

    def grains():
        load_grain.wait()
        grain = gv[...]
        owner = lax.div(lax.div(grain, GRAIN_DEV), n_gy)
        key = owner * GRAIN_DEV + lax.rem(grain, GRAIN_DEV)
        tiles = key.shape[0]
        column = lax.broadcasted_iota(jnp.int32, (tiles, n_gx * GRAIN_DEV), 1)
        chosen = jnp.concatenate(
            [(column == key[:, s : s + 1]).astype(jnp.float32) for s in range(slots)], axis=0
        )
        summed = lax.dot_general(
            chosen, part[...], (((0,), (0,)), ((), ())),
            precision=lax.Precision.HIGHEST, preferred_element_type=jnp.float32,
        )
        gsend[...] = summed.reshape(n_gx, GRAIN_DEV, nz)
        for d in range(1, n_gx):
            grain_exchange(d).start()

    recv(0, 0)
    potential(0)
    send(0, LM)
    send(0, 5, (0, 1))
    over_x(sums)

    def first(s):
        recv(0, s)
        phase(0, s)

    for s in (1, 2, 3):
        first(s)
        send(0, s + 5, (0, 1))
    first(4)
    send(1, 1)
    recv(0, LM)
    density(0)
    send(1, 0)
    for s in (5, 6, 7, 8):
        first(s)
        if s < 7:
            send(1, 2 * s - 8)
            send(1, 2 * s - 7)
        elif s == 7:
            send(1, 6)
    recv(1, 0)
    potential(1)
    send(1, LM)
    send(1, 7)
    send(1, 8)
    grains()

    def second(s):
        recv(1, s)
        phase(1, s)

    second(1)
    second(2)
    second(3)
    second(4)
    recv(1, LM)
    density(1)
    second(5)
    for k in range(fields + 1):
        sent(0, k)
    second(6)
    total = gsend[gx]
    for d in range(1, n_gx):
        grain_exchange(d).wait_recv()
        total += grecv[d]
    grad[...] = total
    for d in range(1, n_gx):
        grain_exchange(d).wait_send()
    second(7)
    for k in (0, 1, 2, 3, 4, 5, 6, LM):
        sent(1, k)
    second(8)
    sent(1, 7)
    sent(1, 8)


def solution(mesh):
    n_gx, n_gy = mesh.shape["gx"], mesh.shape["gy"]

    def shards(cotangent, fields_one, fields_zero, slot_grain):
        fields, cx, cy, nz = cotangent.shape
        whole = pltpu.VMEM((fields, cx, cy, nz), jnp.float32)
        padded = pltpu.VMEM((fields, cx + 2, cy, nz), jnp.float32)
        single = pltpu.VMEM((cx, cy, nz), jnp.float32)
        rows = pltpu.VMEM((2, fields + 1, 2, cx, nz), jnp.float32)
        tiles = cx // TILE * (cy // TILE)
        row_count = tiles * slot_grain.shape[-1]
        far = pl.BlockSpec(memory_space=pltpu.HBM)
        vmem = pl.BlockSpec(memory_space=pltpu.VMEM)
        return pl.pallas_call(
            functools.partial(kernel, n_gx, n_gy),
            out_shape=(
                pltpu.VMEM(cotangent.shape, jnp.float32),
                jax.ShapeDtypeStruct((GRAIN_DEV, nz), jnp.float32),
            ),
            in_specs=[far, far, far, far],
            out_specs=(vmem, vmem),
            scratch_shapes=[
                padded, padded, pltpu.VMEM((2, cx + 2, cy, nz), jnp.float32),
                whole, whole,
                single, single, single, single, single, single,
                rows, rows,
                pltpu.VMEM((row_count, nz), jnp.float32),
                pltpu.VMEM((tiles, slot_grain.shape[-1]), jnp.int32),
                pltpu.VMEM((n_gx, GRAIN_DEV, nz), jnp.float32),
                pltpu.VMEM((n_gx, GRAIN_DEV, nz), jnp.float32),
                pltpu.SemaphoreType.DMA((2, fields + 1, 4)),
                pltpu.SemaphoreType.DMA((2, fields + 1, 4)),
                pltpu.SemaphoreType.DMA((fields + 3,)),
                pltpu.SemaphoreType.DMA((n_gx,)),
                pltpu.SemaphoreType.DMA((n_gx,)),
            ],
            compiler_params=pltpu.CompilerParams(
                collective_id=0, has_side_effects=True, vmem_limit_bytes=48 * 1024 * 1024
            ),
            cost_estimate=pl.CostEstimate(
                flops=100 * cotangent.size, bytes_accessed=16 * cotangent.size, transcendentals=0
            ),
        )(cotangent, fields_one, fields_zero, slot_grain.reshape(tiles, -1))

    placed = (
        P(None, "gx", "gy", None),
        P(None, "gx", "gy", None),
        P(None, "gx", "gy", None),
        P("gx", "gy", None),
    )
    return jax.shard_map(
        shards,
        mesh=mesh,
        in_specs=placed,
        out_specs=(P(None, "gx", "gy", None), P(("gx", "gy"), None)),
        check_vma=False,
    )
```

```python
import functools

import jax
import jax.numpy as jnp
from jax import lax
from jax.experimental import pallas as pl
from jax.experimental.pallas import tpu as pltpu
from jax.sharding import PartitionSpec as P

TILE = 8
GRAIN_DEV = 8
DT = 0.05
MESH = pl.DeviceIdType.MESH
LM = 9


def kernel(
    n_gx, n_gy, cot, f1, f0, slot_grain, out, grad,
    cp, c1p, lmp, f1v, f0v, s1, w1, k1, s0, w2, k2, yh, ys, part, gv, gsend, grecv,
    send_sem, recv_sem, load_sem, gsend_sem, grecv_sem,
):
    fields, cx, cy, nz = cot.shape
    slots = fields - 1
    gx, gy = lax.axis_index("gx"), lax.axis_index("gy")
    can_send = (gx < n_gx - 1, gx > 0, gy < n_gy - 1, gy > 0)
    can_recv = (gx > 0, gx < n_gx - 1, gy > 0, gy < n_gy - 1)
    target = (
        (jnp.minimum(gx + 1, n_gx - 1), gy),
        (jnp.maximum(gx - 1, 0), gy),
        (gx, jnp.minimum(gy + 1, n_gy - 1)),
        (gx, jnp.maximum(gy - 1, 0)),
    )

    barrier = pltpu.get_barrier_semaphore()
    for d in range(1, n_gx):
        pl.semaphore_signal(barrier, inc=1, device_id=(lax.rem(gx + d, n_gx), gy), device_id_type=MESH)
    for side in (2, 3):
        def greet(side=side):
            pl.semaphore_signal(barrier, inc=1, device_id=target[side], device_id_type=MESH)
        pl.when(can_send[side])(greet)
    def load(source, dest, index):
        return pltpu.make_async_copy(source, dest, load_sem.at[index])

    loads = [load(cot.at[k], cp.at[k, pl.ds(1, cx)], k) for k in range(fields)]
    load_f1, load_f0 = load(f1, f1v, fields), load(f0, f0v, fields + 1)
    load_grain = load(slot_grain, gv, fields + 2)
    for copy in loads:
        copy.start()
    load_f1.start()
    load_f0.start()
    load_grain.start()

    def remote(step, k, side):
        if side < 2:
            padded = lmp.at[step] if k == LM else (c1p.at[k] if step else cp.at[k])
            dst = padded.at[0 if side == 0 else cx + 1]
            edge = cx - 1 if side == 0 else 0
            if step == 0 and k != LM:
                src = cot.at[k, edge]
            else:
                src = padded.at[edge + 1]
        else:
            src, dst = ys.at[step, k, side - 2], yh.at[step, k, side - 2]
        return pltpu.make_async_remote_copy(
            src_ref=src, dst_ref=dst, send_sem=send_sem.at[step, k, side],
            recv_sem=recv_sem.at[step, k, side], device_id=target[side], device_id_type=MESH,
        )

    def send(step, k, sides=(0, 1, 2, 3)):
        for side in sides:
            pl.when(can_send[side])(lambda side=side: remote(step, k, side).start())

    def sent(step, k):
        for side in range(4):
            pl.when(can_send[side])(lambda side=side: remote(step, k, side).wait_send())

    def recv(step, k):
        for side in range(4):
            pl.when(can_recv[side])(lambda side=side: remote(step, k, side).wait_recv())

    def clear_x(row):
        zero = jnp.zeros((cy, nz), jnp.float32)

        def body(k, _):
            cp[k, row] = zero
            c1p[k, row] = zero
            return 0

        lax.fori_loop(0, fields, body, 0)
        lmp[0, row] = zero
        lmp[1, row] = zero

    def clear_y(side):
        zero = jnp.zeros((cx, nz), jnp.float32)

        def body(k, _):
            yh[0, k, side] = zero
            yh[1, k, side] = zero
            return 0

        lax.fori_loop(0, fields + 1, body, 0)

    pl.when(gx == 0)(lambda: clear_x(0))
    pl.when(gx == n_gx - 1)(lambda: clear_x(cx + 1))
    pl.when(gy == 0)(lambda: clear_y(0))
    pl.when(gy == n_gy - 1)(lambda: clear_y(1))

    beside = (gy > 0).astype(jnp.int32) + (gy < n_gy - 1).astype(jnp.int32)
    pl.semaphore_wait(barrier, n_gx - 1 + beside)

    for k in range(4):
        send(0, k, (0, 1))

    row_id = lax.broadcasted_iota(jnp.int32, (cy, nz), 0)
    lane_id = lax.broadcasted_iota(jnp.int32, (cy, nz), 1)

    def lap(ref, low, high, x):
        v = ref[x + 1]
        total = ref[x] + ref[x + 2]
        total += jnp.where(row_id == 0, low[pl.ds(x, 1), :], pltpu.roll(v, 1, 0))
        total += jnp.where(row_id == cy - 1, high[pl.ds(x, 1), :], pltpu.roll(v, cy - 1, 0))
        total += jnp.where(lane_id == 0, 0.0, pltpu.roll(v, 1, 1))
        total += jnp.where(lane_id == nz - 1, 0.0, pltpu.roll(v, nz - 1, 1))
        return v, total - 6.0 * v

    def stage(step, k, x, v):
        ys[step, k, 0, pl.ds(x, 1), :] = v[cy - 1 : cy]
        ys[step, k, 1, pl.ds(x, 1), :] = v[0:1]

    def over_x(body, init=0):
        return lax.fori_loop(0, cx, body, init)

    def stage_cot(k):
        loads[k].wait()

        def body(x, _):
            stage(0, k, x, cp[k, x + 1])
            return 0

        over_x(body)
        send(0, k, (2, 3))

    for k in range(fields):
        stage_cot(k)

    def potential(step):
        ref = c1p if step else cp

        def body(x, _):
            _, value = lap(ref.at[0], yh.at[step, 0, 0], yh.at[step, 0, 1], x)
            value = DT * value
            lmp[step, x + 1] = value
            stage(step, LM, x, value)
            return 0

        over_x(body)

    def density(step):
        ref, field, coupled = (c1p, f0v, k2) if step else (cp, f1v, k1)

        def body(x, _):
            lam_mu, lap_mu = lap(lmp.at[step], yh.at[step, LM, 0], yh.at[step, LM, 1], x)
            c = field[0, x]
            curvature = 16.0 * (2.0 - 12.0 * c + 12.0 * c * c) + 2.0
            value = ref[0, x + 1] + lam_mu * curvature - lap_mu - (12.0 * DT) * coupled[x]
            if step:
                out[0, x] = value
            else:
                c1p[0, x + 1] = value
                stage(1, 0, x, value)
            return 0

        over_x(body)

    def phase(step, s):
        ref, field, base, weighted = (c1p, f0v, s0, w2) if step else (cp, f1v, s1, w1)

        def body(x, total):
            v, lap_v = lap(ref.at[s], yh.at[step, s, 0], yh.at[step, s, 1], x)
            eta, c = field[s, x], field[0, x]
            inner = v * (base[x] - 2.0 * (2.0 - c) * eta) + 2.0 * eta * weighted[x]
            value = v - (12.0 * DT) * inner + DT * lap_v
            value += 12.0 * lmp[step, x + 1] * (eta * eta - eta)
            if step:
                out[s, x] = value
                return total
            c1p[s, x + 1] = value
            stage(1, s, x, value)
            old = f0v[s, x]
            first, second = value * old, value * (old * old - old)
            w2[x] = first if s == 1 else w2[x] + first
            k2[x] = second if s == 1 else k2[x] + second
            return total + (v + value)

        if step:
            over_x(body)
        else:
            total = over_x(body, jnp.zeros((cy, nz), jnp.float32))
            rows = jnp.sum(total.reshape(cy // TILE, TILE, nz), axis=1)
            part[pl.ds((s - 1) * (cy // TILE), cy // TILE), :] = DT * rows

    load_f1.wait()
    load_f0.wait()

    def sums(x, _):
        zero = jnp.zeros((cy, nz), jnp.float32)

        def body(s, carry):
            square, square_old, weighted, coupled = carry
            eta, old, lam = f1v[s, x], f0v[s, x], cp[s, x + 1]
            product = lam * eta
            eta_square = eta * eta
            return (square + eta_square, square_old + old * old, weighted + product, coupled + lam * (eta_square - eta))

        square, square_old, weighted, coupled = lax.fori_loop(1, fields, body, (zero, zero, zero, zero))
        s1[x] = (1.0 - f1v[0, x]) + square
        s0[x] = (1.0 - f0v[0, x]) + square_old
        w1[x] = weighted
        k1[x] = coupled
        return 0

    def grain_exchange(d):
        peer = lax.rem(gx + d, n_gx)
        return pltpu.make_async_remote_copy(
            src_ref=gsend.at[peer], dst_ref=grecv.at[d],
            send_sem=gsend_sem.at[d], recv_sem=grecv_sem.at[d],
            device_id=(peer, gy), device_id_type=MESH,
        )

    def grains():
        load_grain.wait()
        grain = gv[...]
        owner = lax.div(lax.div(grain, GRAIN_DEV), n_gy)
        key = owner * GRAIN_DEV + lax.rem(grain, GRAIN_DEV)
        tiles = key.shape[0]
        column = lax.broadcasted_iota(jnp.int32, (tiles, n_gx * GRAIN_DEV), 1)
        chosen = jnp.concatenate(
            [(column == key[:, s : s + 1]).astype(jnp.float32) for s in range(slots)], axis=0
        )
        summed = lax.dot_general(
            chosen, part[...], (((0,), (0,)), ((), ())),
            precision=lax.Precision.HIGHEST, preferred_element_type=jnp.float32,
        )
        gsend[...] = summed.reshape(n_gx, GRAIN_DEV, nz)
        for d in range(1, n_gx):
            grain_exchange(d).start()

    recv(0, 0)
    potential(0)
    send(0, LM)
    send(0, 4, (0, 1))
    over_x(sums)

    def first(s):
        recv(0, s)
        phase(0, s)

    for s in (1, 2, 3, 4):
        first(s)
        send(0, s + 4, (0, 1))
    recv(0, LM)
    density(0)
    send(1, 0)
    for s in (5, 6, 7, 8):
        first(s)
        send(1, s - 4)
    recv(1, 0)
    potential(1)
    send(1, LM)
    send(1, 5)
    grains()

    def second(s):
        recv(1, s)
        phase(1, s)

    second(1)
    send(1, 6)
    second(2)
    send(1, 7)
    second(3)
    send(1, 8)
    second(4)
    recv(1, LM)
    density(1)
    second(5)
    for k in range(fields + 1):
        sent(0, k)
    second(6)
    total = gsend[gx]
    for d in range(1, n_gx):
        grain_exchange(d).wait_recv()
        total += grecv[d]
    grad[...] = total
    for d in range(1, n_gx):
        grain_exchange(d).wait_send()
    second(7)
    for k in (0, 1, 2, 3, 4, 5, 6, LM):
        sent(1, k)
    second(8)
    sent(1, 7)
    sent(1, 8)


def solution(mesh):
    n_gx, n_gy = mesh.shape["gx"], mesh.shape["gy"]

    def shards(cotangent, fields_one, fields_zero, slot_grain):
        fields, cx, cy, nz = cotangent.shape
        whole = pltpu.VMEM((fields, cx, cy, nz), jnp.float32)
        padded = pltpu.VMEM((fields, cx + 2, cy, nz), jnp.float32)
        single = pltpu.VMEM((cx, cy, nz), jnp.float32)
        rows = pltpu.VMEM((2, fields + 1, 2, cx, nz), jnp.float32)
        tiles = cx // TILE * (cy // TILE)
        row_count = tiles * slot_grain.shape[-1]
        far = pl.BlockSpec(memory_space=pltpu.HBM)
        vmem = pl.BlockSpec(memory_space=pltpu.VMEM)
        return pl.pallas_call(
            functools.partial(kernel, n_gx, n_gy),
            out_shape=(
                pltpu.VMEM(cotangent.shape, jnp.float32),
                jax.ShapeDtypeStruct((GRAIN_DEV, nz), jnp.float32),
            ),
            in_specs=[far, far, far, far],
            out_specs=(vmem, vmem),
            scratch_shapes=[
                padded, padded, pltpu.VMEM((2, cx + 2, cy, nz), jnp.float32),
                whole, whole,
                single, single, single, single, single, single,
                rows, rows,
                pltpu.VMEM((row_count, nz), jnp.float32),
                pltpu.VMEM((tiles, slot_grain.shape[-1]), jnp.int32),
                pltpu.VMEM((n_gx, GRAIN_DEV, nz), jnp.float32),
                pltpu.VMEM((n_gx, GRAIN_DEV, nz), jnp.float32),
                pltpu.SemaphoreType.DMA((2, fields + 1, 4)),
                pltpu.SemaphoreType.DMA((2, fields + 1, 4)),
                pltpu.SemaphoreType.DMA((fields + 3,)),
                pltpu.SemaphoreType.DMA((n_gx,)),
                pltpu.SemaphoreType.DMA((n_gx,)),
            ],
            compiler_params=pltpu.CompilerParams(
                collective_id=0, has_side_effects=True, vmem_limit_bytes=48 * 1024 * 1024
            ),
            cost_estimate=pl.CostEstimate(
                flops=100 * cotangent.size, bytes_accessed=16 * cotangent.size, transcendentals=0
            ),
        )(cotangent, fields_one, fields_zero, slot_grain.reshape(tiles, -1))

    placed = (
        P(None, "gx", "gy", None),
        P(None, "gx", "gy", None),
        P(None, "gx", "gy", None),
        P("gx", "gy", None),
    )
    return jax.shard_map(
        shards,
        mesh=mesh,
        in_specs=placed,
        out_specs=(P(None, "gx", "gy", None), P(("gx", "gy"), None)),
        check_vma=False,
    )
```
